512 devices in a mesh: ctx: 64 (over y, x, core), head: 8 (over z).
Axes of the slice: x: 4, y: 8, z: 8, core: 2. Of those that a mesh axis runs over, the one named last changes fastest.
Arguments:
- query_rows: bfloat16 [16384, 5120], P('ctx', 'head'), may hold values from -7.5 to 7.5
- gate_rows: bfloat16 [16384, 5120], P('ctx', 'head'), may hold values from -4 to 12
- value_rows: bfloat16 [16384, 5120], P('ctx', 'head'), may hold values from -6 to 6
- upstream_rows: bfloat16 [16384, 5120], P('ctx', 'head'), may hold values from -6 to 6
- row_map: int32 [16384], P('ctx'), may hold values from 0 to 16383, as said below
- doc_lengths: int32 [64], replicated, may hold values from 1 to 2048, 16384 in all
- entry_state: float32 [64, 40, 128, 128], P('ctx', 'head'), may hold values from -1.75 to 1.75
- lower_bound: float32 [5120], P('head'), may hold values from 0.3 to 0.7
- norm_gain: float32 [5120], P('head'), may hold values from 0.1 to 1.9
Outputs:
- query_grad: bfloat16 [16384, 5120], P('ctx', 'head')
- gate_grad: bfloat16 [16384, 5120], P('ctx', 'head')
- value_grad: bfloat16 [16384, 5120], P('ctx', 'head')
The draws below stay inside these ranges and needn't reach their ends.
Inputs may be any that keep to these rules, and one draw needn't show every extreme that they name: `row_map`: every loader row appears exactly once; the 256 rows of one balanced shard take at most 8 rows from any one loader shard, and that most is reached. `doc_lengths`: the lengths sum to 16384.
All inputs are finite; a program needn't handle non-finite values.
Results may differ from the reference program's by a relative error of at most 0.0022.
Values may be sent and summed in bfloat16 or wider, within the bound.
A program may use at most 128 MiB of HBM per device.

```python
import math
import jax
import jax.numpy as jnp
import numpy as np
from jax import lax

HEADS = 40
KEY = 128
VAL = 128
TOK_DEV = 256
BLOCK = 128
TOKEN_ROWS = 16384
DOC_MOST = 2048
DOCS = 64
CLOSED_ROWS = 16
N_CTX = 64


def draw_query_rows(key, part):
    key = jax.random.fold_in(key, 3)
    key_base = jax.random.fold_in(key, 0)
    columns = HEADS * KEY
    head_pos = (jnp.arange(columns) // KEY).astype(jnp.float32) / max(HEADS - 1, 1)
    head_lift = 0.6 * 3.0 ** head_pos
    drawn = jnp.clip(jax.random.normal(key_base, (TOKEN_ROWS, columns), jnp.float32), -4.0, 4.0)
    sampled_rows = drawn * head_lift[None, :]
    return sampled_rows.astype(jnp.bfloat16)


def draw_gate_rows(key, part):
    key = jax.random.fold_in(key, 5)
    level_key, noise_key, closure_key = jax.random.split(key, 3)
    columns = HEADS * KEY
    gate_levels = jax.random.uniform(level_key, (columns,), jnp.float32, 3.0, 9.0)
    coarse_jitter = 0.8 * jnp.clip(jax.random.normal(noise_key, (TOKEN_ROWS, columns), jnp.float32), -3.0, 3.0)
    closure_rows = jax.random.randint(closure_key, (CLOSED_ROWS,), 0, TOKEN_ROWS)
    closure_found = jnp.any(jnp.arange(TOKEN_ROWS)[:, None] == closure_rows[None, :], axis=1)
    sampled_rows = jnp.where(closure_found[:, None], -3.0 + 0.3 * coarse_jitter, gate_levels[None, :] + coarse_jitter)
    return sampled_rows.astype(jnp.bfloat16)


def draw_row_map(key, part):
    key = jax.random.fold_in(key, 7)
    key_a, key_b, key_c, key_d, key_e = jax.random.split(key, 5)
    shard_count = N_CTX
    row_count = TOK_DEV
    even_share = row_count // shard_count
    surplus = jax.random.randint(key_a, (shard_count // 2,), 0, even_share + 1).at[0].set(even_share)
    offsets = jnp.concatenate([surplus, -surplus])[jax.random.permutation(key_b, shard_count)]
    rotation = jax.random.permutation(key_c, shard_count)
    peer_ids = jnp.arange(shard_count)
    counts = even_share + offsets[(peer_ids[:, None] + rotation[None, :]) % shard_count]
    count_ends = jnp.cumsum(counts, axis=1)
    row_ids = jnp.arange(row_count)
    dest = jnp.sum((row_ids[None, :, None] >= count_ends[:, None, :]).astype(jnp.int32), axis=2)
    within = row_ids[None, :] - jnp.take_along_axis(count_ends - counts, dest, axis=1)
    col_start = jnp.cumsum(counts, axis=0) - counts
    target = dest * row_count + jnp.take_along_axis(col_start, dest, axis=1) + within
    shuffle = jax.vmap(lambda item: jax.random.permutation(item, row_count))(jax.random.split(key_d, shard_count))
    loader = peer_ids[:, None] * row_count + shuffle
    row_table = jnp.zeros((TOKEN_ROWS,), jnp.int32).at[target.reshape(-1)].set(loader.reshape(-1).astype(jnp.int32))
    reorder = jax.vmap(lambda item: jax.random.permutation(item, row_count))(jax.random.split(key_e, shard_count))
    row_table = jnp.take_along_axis(row_table.reshape(shard_count, row_count), reorder, axis=1)
    return row_table.reshape(-1).astype(jnp.int32)


def levels(stream_key, dims, cuts, smallest, largest):
    gain = 1.0
    for axis_at, shards_of in cuts:
        steps = jax.random.uniform(jax.random.fold_in(jax.random.fold_in(stream_key, 6), axis_at), (shards_of,), jnp.float32, smallest / len(cuts), largest / len(cuts))
        gain = gain * jnp.repeat(jnp.exp(steps), dims[axis_at] // shards_of).reshape((-1,) + (1,) * (len(dims) - 1 - axis_at))
    return gain


def split_up(count, total, most, lean):
    loads = [(1 << 20) // math.isqrt(standing ** lean) + 1 for standing in range(2, count + 1)]
    spare, holding = total - most - (count - 1), [1] * (count - 1)
    while spare > 0:
        movable = [i for i in range(count - 1) if holding[i] < most]
        mass, remaining = sum([loads[i] for i in movable]), spare
        for i in movable:
            addition = min(most - holding[i], max(1, remaining * loads[i] // mass), spare)
            holding[i] = holding[i] + addition
            spare = spare - addition
    return np.array([most] + holding)


def uneven_parts(stream_key, amount, total, most, lean):
    if amount == 2:
        one = jax.random.randint(stream_key, (), max(1, total - most), min(most, total - 1) + 1)
        return jnp.stack([one, total - one])
    lengths = jnp.asarray(split_up(amount, total, most, lean), jnp.int32)
    pairs = (amount - 1) // 2
    source_of, receiver = lengths[1:1 + 2 * pairs:2], lengths[2:2 + 2 * pairs:2]
    room = jnp.minimum(source_of - 1, most - receiver)
    shifted = jax.random.randint(jax.random.fold_in(stream_key, 1), (pairs,), 0, 1 << 20) % (room + 1)
    lengths = lengths.at[1:1 + 2 * pairs:2].set(source_of - shifted).at[2:2 + 2 * pairs:2].set(receiver + shifted)
    return lengths[jax.random.permutation(jax.random.fold_in(stream_key, 2), amount)]


def normal_values(own_key, shape, scale, reach, shards=(), kind=jnp.bfloat16):
    values = scale * jax.random.normal(own_key, shape, jnp.float32)
    if shards:
        values = values * levels(own_key, shape, shards, -0.22, 0.18)
    return jnp.clip(values, -reach, reach).astype(kind)


def setup_inputs(seed: int = 0) -> dict:
    streams_of = jax.random.split(jax.random.key(seed), 10)
    return {
        "query_rows": draw_query_rows(jax.random.fold_in(streams_of[9], 71), 0),
        "gate_rows": draw_gate_rows(jax.random.fold_in(streams_of[9], 71), 0),
        "value_rows": normal_values(streams_of[2], (TOKEN_ROWS, HEADS * VAL), 1.0, 6.0, ((0, 64), (1, 8))),
        "upstream_rows": normal_values(streams_of[3], (TOKEN_ROWS, HEADS * VAL), 1.0, 6.0, ((0, 64), (1, 8))),
        "row_map": draw_row_map(jax.random.fold_in(streams_of[9], 71), 0),
        "doc_lengths": uneven_parts(streams_of[5], DOCS, TOKEN_ROWS, DOC_MOST, 2).astype(jnp.int32),
        "entry_state": normal_values(streams_of[6], (N_CTX, HEADS, KEY, VAL), 0.3, 1.75, ((0, 64), (1, 8)), jnp.float32),
        "lower_bound": jnp.clip(0.3 + 0.39999998 * jax.random.uniform(streams_of[7], (HEADS * KEY,), jnp.float32) ** levels(streams_of[7], (HEADS * KEY,), ((0, 8),), -0.2, 0.2), 0.3, 0.7),
        "norm_gain": jnp.clip(1.0 + 0.18 * jax.random.normal(streams_of[8], (HEADS * VAL,), jnp.float32), 0.1, 1.9),
    }


TOP_PRECISION = lax.Precision.HIGHEST
EPSILON = 1e-06

def block_prep(gate_pre, starts, bounds):
    opened = jax.nn.sigmoid(gate_pre)
    forgets = bounds + (1.0 - bounds) * opened
    stored_rows = 1.0 - forgets
    decay_log = jnp.cumsum(jnp.log(forgets), axis=0)
    segment = jnp.cumsum(starts.astype(jnp.int32))
    row_ids = jnp.arange(starts.shape[0])
    shared_document = ((segment[:, None] == segment[None, :]) & (row_ids[:, None] >= row_ids[None, :])).astype(jnp.float32)
    carry_valid = (segment == 0).astype(jnp.float32)
    last_doc = (segment == segment[-1]).astype(jnp.float32)
    return (opened, forgets, stored_rows, decay_log, shared_document, carry_valid, last_doc)

def block_forward(prep, queries, value_matrix, incoming_state):
    opened, forgets, stored_rows, decay_log, shared_document, carry_valid, last_doc = prep
    query_decayed = queries * jnp.exp(decay_log)
    key_dec = stored_rows * jnp.exp(-decay_log)
    scores = jnp.einsum('thk,shk->hts', query_decayed, key_dec, precision=TOP_PRECISION) * shared_document[None]
    output_rows = jnp.einsum('hts,shv->thv', scores, value_matrix, precision=TOP_PRECISION)
    output_rows = output_rows + carry_valid[:, None, None] * jnp.einsum('dfb,fbu->dfu', query_decayed, incoming_state, precision=TOP_PRECISION)
    trailing_key = stored_rows * jnp.exp(decay_log[-1] - decay_log) * last_doc[:, None, None]
    outgoing_state = (carry_valid[-1] * jnp.exp(decay_log[-1]))[:, :, None] * incoming_state
    outgoing_state = outgoing_state + jnp.einsum('lei,len->ein', trailing_key, value_matrix, precision=TOP_PRECISION)
    return (output_rows, outgoing_state)

def block_backward(prep, queries, value_matrix, upstream_gradient, incoming_state, state_end, incoming_carry, bounds):
    opened, forgets, stored_rows, decay_log, shared_document, carry_valid, last_doc = prep
    query_decayed = queries * jnp.exp(decay_log)
    key_dec = stored_rows * jnp.exp(-decay_log)
    scores = jnp.einsum('thk,shk->hts', query_decayed, key_dec, precision=TOP_PRECISION) * shared_document[None]
    weights = jnp.einsum('thv,shv->hts', upstream_gradient, value_matrix, precision=TOP_PRECISION) * shared_document[None]
    query_gradient = jnp.einsum('hts,shk->thk', weights, key_dec, precision=TOP_PRECISION)
    query_gradient = query_gradient + carry_valid[:, None, None] * jnp.einsum('crp,ryp->cry', upstream_gradient, incoming_state, precision=TOP_PRECISION)
    query_gradient = jnp.exp(decay_log) * query_gradient
    trailing_decay = jnp.exp(decay_log[-1] - decay_log) * last_doc[:, None, None]
    value_gradient = jnp.einsum('hts,thv->shv', scores, upstream_gradient, precision=TOP_PRECISION)
    value_gradient = value_gradient + jnp.einsum('ijo,jof->ijf', stored_rows * trailing_decay, incoming_carry, precision=TOP_PRECISION)
    key_gradient = jnp.exp(-decay_log) * jnp.einsum('hts,thk->shk', weights, query_decayed, precision=TOP_PRECISION)
    key_gradient = key_gradient + trailing_decay * jnp.einsum('dio,ico->dic', value_matrix, incoming_carry, precision=TOP_PRECISION)
    mixture = queries * query_gradient - stored_rows * key_gradient
    grad_log = jnp.einsum('ts,thk->shk', shared_document, mixture, precision=TOP_PRECISION)
    grad_log = grad_log + last_doc[:, None, None] * lax.optimization_barrier(jnp.sum(incoming_carry * state_end, axis=2))[None]
    grad_gate = (grad_log / forgets - key_gradient) * (1.0 - bounds) * opened * (1.0 - opened)
    returned_gradient = carry_valid[0] * jnp.einsum('o,oza,ozn->zan', shared_document[:, 0], query_decayed, upstream_gradient, precision=TOP_PRECISION)
    returned_gradient = returned_gradient + (carry_valid[0] * last_doc[0] * jnp.exp(decay_log[-1]))[:, :, None] * incoming_carry
    return (query_gradient, grad_gate, value_gradient, returned_gradient)

def by_block(array):
    return array.reshape((array.shape[0] // BLOCK, BLOCK) + array.shape[1:])

def unblock(array):
    return array.reshape((-1,) + array.shape[2:])

def shard_forward(queries, gate_pre, value_matrix, starts, bounds, entry):

    def block_step(incoming_state, pieces):
        query_blk, gate_blk, value_blk, start_blk = pieces
        prep = block_prep(gate_blk, start_blk, bounds)
        output_rows, outgoing_state = block_forward(prep, query_blk, value_blk, incoming_state)
        return (outgoing_state, (output_rows, incoming_state, outgoing_state))
    pieces = (by_block(queries), by_block(gate_pre), by_block(value_matrix), by_block(starts))
    _, (output_rows, states_in, states_end) = lax.scan(block_step, entry, pieces)
    return (unblock(output_rows), states_in, states_end)

def shard_backward(queries, gate_pre, value_matrix, starts, bounds, upstream_gradient, states_in, states_end, carry):

    def block_step(incoming_carry, pieces):
        query_blk, gate_blk, value_blk, start_blk, up_blk, in_blk, end_blk = pieces
        prep = block_prep(gate_blk, start_blk, bounds)
        query_gradient, grad_gate, value_gradient, returned_gradient = block_backward(prep, query_blk, value_blk, up_blk, in_blk, end_blk, incoming_carry, bounds)
        return (returned_gradient, (query_gradient, grad_gate, value_gradient))
    pieces = (by_block(queries), by_block(gate_pre), by_block(value_matrix), by_block(starts), by_block(upstream_gradient), states_in, states_end)
    returned_gradient, (query_gradient, grad_gate, value_gradient) = lax.scan(block_step, carry, pieces, reverse=True)
    return (unblock(query_gradient), unblock(grad_gate), unblock(value_gradient), returned_gradient)

def norm_grad(output_rows, upstream_y, gains, row_squares, row_cross):
    inverse = lax.rsqrt(row_squares / (HEADS * VAL) + EPSILON)[..., None, None]
    return inverse * gains * upstream_y - output_rows * inverse ** 3 * (row_cross / (HEADS * VAL))[..., None, None]

def reference(query_rows, gate_rows, value_rows, upstream_rows, row_map, doc_lengths, entry_state, lower_bound, norm_gain):

    def balanced(array, width):
        return jnp.take(array, row_map, axis=0).astype(jnp.float32).reshape(N_CTX, TOK_DEV, HEADS, width)
    queries = balanced(query_rows, KEY)
    gate_pre = balanced(gate_rows, KEY)
    value_matrix = balanced(value_rows, VAL)
    upstream_y = balanced(upstream_rows, VAL)
    positions = jnp.arange(TOKEN_ROWS).astype(jnp.int32)
    doc_ends = jnp.cumsum(doc_lengths).astype(jnp.int32)
    starts = (positions == 0) | jnp.any(positions[:, None] == doc_ends[None, :-1], axis=1)
    starts = starts.reshape(N_CTX, TOK_DEV)
    bounds = lower_bound.reshape(HEADS, KEY)
    gains = norm_gain.reshape(HEADS, VAL)

    def forward_one(pieces):
        return shard_forward(pieces[0], pieces[1], pieces[2], pieces[3], bounds, pieces[4])
    output_rows, states_in, states_end = lax.map(forward_one, (queries, gate_pre, value_matrix, starts, entry_state))
    row_squares = lax.optimization_barrier(jnp.sum(output_rows * output_rows, axis=(2, 3)))
    row_cross = lax.optimization_barrier(jnp.sum(gains * upstream_y * output_rows, axis=(2, 3)))
    upstream_gradient = norm_grad(output_rows, upstream_y, gains, row_squares, row_cross)

    def shard_step(carry, pieces):
        query_gradient, grad_gate, value_gradient, returned_gradient = shard_backward(pieces[0], pieces[1], pieces[2], pieces[3], bounds, pieces[4], pieces[5], pieces[6], carry)
        return (returned_gradient, (query_gradient, grad_gate, value_gradient))
    zero_state = jnp.zeros((HEADS, KEY, VAL), jnp.float32)
    _, (query_gradient, grad_gate, value_gradient) = lax.scan(shard_step, zero_state, (queries, gate_pre, value_matrix, starts, upstream_gradient, states_in, states_end), reverse=True)

    def home(grad):
        flat = grad.reshape(TOKEN_ROWS, grad.shape[2] * grad.shape[3])
        return jnp.zeros(flat.shape, jnp.float32).at[row_map].set(flat).astype(jnp.bfloat16)
    return (home(query_gradient), home(grad_gate), home(value_gradient))
```

```python
import functools

import jax
import jax.numpy as jnp
from jax import lax
from jax.experimental import pallas as pl
from jax.experimental.pallas import tpu as pltpu
from jax.sharding import PartitionSpec as P

BLOCK = 128
LANES = 128
DOC_MOST = 2048
EPSILON = 1e-06
MESH = pl.DeviceIdType.MESH
BF = jnp.bfloat16
F32 = jnp.float32
NN = (((1,), (0,)), ((), ()))
NT = (((1,), (1,)), ((), ()))


def dot(a, b, dims):
    return lax.dot_general(a, b, dims, preferred_element_type=F32)


def cat(parts, axis):
    return jnp.concatenate(parts, axis=axis)


def halves(x):
    high = x.astype(BF)
    return high, (x - high.astype(F32)).astype(BF)


def thirds(x):
    high = x.astype(BF)
    rest = x - high.astype(F32)
    middle = rest.astype(BF)
    return high, middle, (rest - middle.astype(F32)).astype(BF)


def nn3(a, b):
    return dot(cat([a[0], a[0], a[1]], 1), cat([b[0], b[1], b[0]], 0), NN)


def nt3(a, b):
    return dot(cat([a[0], a[0], a[1]], 1), cat([b[0], b[1], b[0]], 1), NT)


def nn2(a, exact):
    return dot(cat(a, 1), cat([exact, exact], 0), NN)


def nt2(a, exact):
    return dot(cat(a, 1), cat([exact, exact], 1), NT)


def exact_nn2(exact, b):
    return dot(cat([exact, exact], 1), cat(b, 0), NN)


def iota(shape, axis):
    return lax.broadcasted_iota(jnp.int32, shape, axis)


def one(mask):
    return jnp.where(mask, 1.0, 0.0).astype(F32)


def column(row):
    parts = [
        jnp.broadcast_to(row[:, at : at + LANES], (LANES, LANES)).T
        for at in range(0, row.shape[1], LANES)
    ]
    return cat(parts, 0) if len(parts) > 1 else parts[0]


def widen(col, width):
    return cat([col] * (width // LANES), 1)


def peer(me, k, count):
    if count != 64:
        return lax.rem(me + k, count)
    dy, rest = lax.rem(k, 8), lax.div(k, 8)
    dx, dc = lax.div(rest, 2), lax.rem(rest, 2)
    y = lax.rem(lax.div(me, 8) + dy, 8)
    x = lax.rem(lax.rem(lax.div(me, 2), 4) + dx, 4)
    core = lax.rem(lax.rem(me, 2) + dc, 2)
    return (y * 4 + x) * 2 + core


def kernel(
    sizes,
    small_ref,
    q_ref,
    p_ref,
    v_ref,
    y_ref,
    entry_ref,
    bound_ref,
    gain_ref,
    dq_ref,
    dp_ref,
    dv_ref,
    req_send,
    req_recv,
    row_send,
    row_recv,
    dq_send,
    dq_recv,
    dvp_send,
    dvp_recv,
    sum_send,
    sum_recv,
    tot_send,
    tot_recv,
    car_send,
    car_recv,
    stat_send,
    stat_recv,
    gather_ref,
    settle_ref,
    place_ref,
    back_ref,
    shared_ref,
    shared_t_ref,
    valid_ref,
    last_ref,
    through_ref,
    q_bal,
    v_bal,
    y_bal,
    sig_ref,
    forget_ref,
    store_ref,
    eq_ref,
    ek_ref,
    tail_ref,
    qd_ref,
    kd_ref,
    score_ref,
    weight_ref,
    state_ref,
    factor_ref,
    back_state_ref,
    out_ref,
    dq_bal,
    dk_bal,
    dv_bal,
    square_ref,
    cross_ref,
    send_sem,
    recv_sem,
):
    count, head_count, rows, heads, cap, group, chunks = sizes
    slots = count * cap
    blocks = rows // BLOCK
    part = LANES // group
    me = lax.axis_index("ctx")
    plane = lax.axis_index("head")
    base = me * rows

    def to_ctx(src, dst, sem, d):
        return pltpu.make_async_remote_copy(
            src_ref=src,
            dst_ref=dst,
            send_sem=send_sem.at[sem],
            recv_sem=recv_sem.at[sem],
            device_id={"ctx": d},
            device_id_type=MESH,
        )

    def drain(view, sems, sem):
        pltpu.make_async_copy(view, view, sems.at[sem]).wait()

    REQ, STAT, SUM, TOT, CAR, DQ, ROWS = 0, 1, 2, 3, 4, 5, 6
    DVP = ROWS + len(chunks)

    barrier = pltpu.get_barrier_semaphore()

    def greet(k, carry):
        pl.semaphore_signal(
            barrier, inc=1, device_id={"ctx": peer(me, k, count)}, device_id_type=MESH
        )
        return carry

    def greet_plane(k, carry):
        pl.semaphore_signal(
            barrier,
            inc=1,
            device_id={"head": lax.rem(plane + k, head_count)},
            device_id_type=MESH,
        )
        return carry

    lax.fori_loop(1, count, greet, 0)
    lax.fori_loop(1, head_count, greet_plane, 0)

    small = small_ref[...].astype(F32)
    map_row = cat([small[b : b + 1] for b in range(blocks)], 1)
    source_row = jnp.floor(map_row * (1.0 / rows))
    local_row = map_row - source_row * rows
    source_col = column(source_row)
    local_col = column(local_row)
    same = (widen(source_col, rows) == source_row) & (
        iota((rows, rows), 0) < iota((rows, rows), 1)
    )
    rank_row = jnp.sum(one(same), axis=0, keepdims=True)
    slot_row = source_row * cap + rank_row
    slot_col = column(slot_row)
    back_ref[...] = one(iota((slots, rows), 0).astype(F32) == slot_row).astype(BF)
    place_ref[...] = one(
        iota((rows, slots), 1).astype(F32) == widen(slot_col, slots)
    ).astype(BF)
    asked_mine = dot(back_ref[...], (local_col + 1.0).astype(BF), NN) - 1.0
    req_send[...] = asked_mine.reshape(count, cap, LANES)

    pl.semaphore_wait(barrier, count - 1 + head_count - 1)

    def ask(k, carry):
        d = peer(me, k, count)
        to_ctx(req_send.at[d], req_recv.at[me], REQ, d).start()
        return carry

    lax.fori_loop(1, count, ask, 0)
    req_recv[me] = req_send[me]

    length_col = column(small[blocks : blocks + 1])
    ends_row = jnp.sum(
        jnp.where(iota((LANES, LANES), 0) <= iota((LANES, LANES), 1), length_col, 0.0),
        axis=0,
        keepdims=True,
    )
    ends_col = column(ends_row)
    position = (iota((1, rows), 1) + base).astype(F32)
    document_row = jnp.sum(one(widen(ends_col, rows) <= position), axis=0, keepdims=True)
    document_col = column(document_row)
    before = (iota((1, LANES), 1) * 0 + (base - 1)).astype(F32)
    before = jnp.where(
        before < 0.0, -1.0, jnp.sum(one(ends_col <= before), axis=0, keepdims=True)
    )
    for b in range(blocks):
        at = slice(b * BLOCK, (b + 1) * BLOCK)
        previous = before if b == 0 else document_col[b * BLOCK - 1 : b * BLOCK]
        final = document_col[(b + 1) * BLOCK - 1 : (b + 1) * BLOCK]
        alike = document_col[at] == document_row[:, at]
        earlier = iota((BLOCK, BLOCK), 0) >= iota((BLOCK, BLOCK), 1)
        later = iota((BLOCK, BLOCK), 0) <= iota((BLOCK, BLOCK), 1)
        shared_ref[b] = one(alike & earlier)
        shared_t_ref[b] = one(alike & later)
        valid_ref[b] = one(document_col[at] == previous)
        last_ref[b] = one(document_col[at] == final)
        through_ref[pl.ds(b, 1)] = one(previous == final)

    def wait_all(view, sem):
        drain(view, recv_sem, sem)

    wait_all(req_recv.at[pl.ds(0, count - 1)], REQ)
    asked = req_recv[...].reshape(slots, LANES)
    gather = cat(
        [
            one(asked == (iota((slots, LANES), 1) + b * LANES).astype(F32))
            for b in range(blocks)
        ],
        1,
    )
    gather_ref[...] = gather.astype(BF)

    step_slots = min(slots, 128)
    step_peers = step_slots // cap
    for number, (first, past) in enumerate(chunks):

        def pack(h, carry):
            at = pl.ds(pl.multiple_of(h * LANES, LANES), LANES)
            wide = cat([q_ref[:, at], p_ref[:, at], v_ref[:, at], y_ref[:, at]], 1)
            for piece in range(slots // step_slots):
                picked = dot(
                    gather_ref[piece * step_slots : (piece + 1) * step_slots], wide, NN
                )
                slab = cat(
                    [
                        picked[:, a * LANES : (a + 1) * LANES].reshape(step_peers, cap, LANES)
                        for a in range(4)
                    ],
                    1,
                )
                row_send[h, piece * step_peers : (piece + 1) * step_peers] = slab.astype(BF)
            return carry

        lax.fori_loop(first, past, pack, 0)

        def serve(k, carry):
            d = peer(me, k, count)
            span = pl.ds(first, past - first)
            to_ctx(row_send.at[span, d], row_recv.at[span, me], ROWS + number, d).start()
            return carry

        lax.fori_loop(1, count, serve, 0)

    def own(h, carry):
        row_recv[h, me] = row_send[h, me]
        return carry

    lax.fori_loop(0, heads, own, 0)
    settle_ref[...] = gather.T.astype(BF)

    square_ref[...] = jnp.zeros_like(square_ref)
    cross_ref[...] = jnp.zeros_like(cross_ref)
    lower = one(iota((BLOCK, BLOCK), 0) >= iota((BLOCK, BLOCK), 1)).astype(BF)
    lower3 = cat([lower, lower, lower], 1)

    def unslab(slab, parts):
        wide = slab.astype(F32)
        return cat(
            [
                wide[:, a * cap : (a + 1) * cap].reshape(slots, LANES).astype(BF)
                for a in range(parts)
            ],
            1,
        )

    def forward(h, carry):
        balanced = dot(place_ref[...], unslab(row_recv[h], 4), NN)
        bound = bound_ref[pl.ds(h, 1)]
        gain = gain_ref[pl.ds(h, 1)]
        state = entry_ref[0, h].T
        for b in range(blocks):
            at = slice(b * BLOCK, (b + 1) * BLOCK)
            q, p, v, y = [balanced[at, a * LANES : (a + 1) * LANES] for a in range(4)]
            v_exact = v.astype(BF)
            sig = jax.nn.sigmoid(p)
            forget = bound + (1.0 - bound) * sig
            store = 1.0 - forget
            decay = dot(lower3, cat(thirds(jnp.log(forget)), 0), NN)
            total = decay[BLOCK - 1 : BLOCK]
            eq = jnp.exp(decay)
            ek = jnp.exp(-decay)
            tail = jnp.exp(total - decay) * last_ref[b]
            factor = through_ref[pl.ds(b, 1)] * jnp.exp(total)
            qd = q * eq
            kd = store * ek
            qd2 = halves(qd)
            scores = nt3(qd2, halves(kd)) * shared_ref[b]
            out = nn2(halves(scores), v_exact) + valid_ref[b] * nt3(qd2, halves(state))
            state_ref[h, b] = state
            state = state * factor + exact_nn2(v.T.astype(BF), halves(store * tail))
            square_ref[at] += out * out
            cross_ref[at] += gain * y * out
            q_bal[h, b] = q.astype(BF)
            v_bal[h, b] = v_exact
            y_bal[h, b] = y.astype(BF)
            sig_ref[h, b] = sig
            forget_ref[h, b] = forget
            store_ref[h, b] = store
            eq_ref[h, b] = eq
            ek_ref[h, b] = ek
            tail_ref[h, b] = tail
            qd_ref[h, b] = qd
            kd_ref[h, b] = kd
            score_ref[h, b] = scores
            factor_ref[h, b] = factor
            out_ref[h, b] = out
        state_ref[h, blocks] = state
        return carry

    for number, (first, past) in enumerate(chunks):
        wait_all(
            row_recv.at[pl.ds(first, past - first), pl.ds(0, count - 1)], ROWS + number
        )
        lax.fori_loop(first, past, forward, 0)

    ones = jnp.ones((8, 3 * LANES), BF)
    squares = dot(ones, cat(thirds(square_ref[...]), 1), NT)
    crosses = dot(ones, cat(thirds(cross_ref[...]), 1), NT)
    stat_send[...] = jnp.where(iota((8, rows), 0) < 4, squares, crosses)

    def share(k, carry):
        pltpu.make_async_remote_copy(
            src_ref=stat_send,
            dst_ref=stat_recv.at[plane],
            send_sem=send_sem.at[STAT],
            recv_sem=recv_sem.at[STAT],
            device_id={"head": lax.rem(plane + k, head_count)},
            device_id_type=MESH,
        ).start()
        return carry

    lax.fori_loop(1, head_count, share, 0)
    stat_recv[plane] = stat_send[...]
    sum_send[...] = jnp.zeros_like(sum_send)
    if head_count > 1:
        wait_all(stat_recv.at[pl.ds(0, head_count - 1)], STAT)
    stats = jnp.sum(stat_recv[...], axis=0)
    width = float(head_count * heads * LANES)
    inverse = lax.rsqrt(stats[0:1] / width + EPSILON)
    slope = inverse * inverse * inverse * (stats[4:5] / width)
    square_ref[...] = column(inverse)
    cross_ref[...] = column(slope)

    def summarize(h, carry):
        gain = gain_ref[pl.ds(h, 1)]
        back = []
        for b in range(blocks):
            at = slice(b * BLOCK, (b + 1) * BLOCK)
            g = square_ref[at] * gain * y_bal[h, b].astype(F32) - out_ref[h, b] * cross_ref[at]
            out_ref[h, b] = g
            back.append(nn3(halves((g * valid_ref[b]).T), halves(qd_ref[h, b])))
            back_state_ref[h, b] = back[b]
        summary = back[blocks - 1]
        decay = factor_ref[h, blocks - 1]
        for b in reversed(range(blocks - 1)):
            summary = back[b] + factor_ref[h, b] * summary
            decay = decay * factor_ref[h, b]
        sum_send[:, h] = summary.reshape(group, part, LANES)
        sum_send[:, heads, pl.ds(h, 1)] = jnp.broadcast_to(decay[None], (group, 1, LANES))
        return carry

    lax.fori_loop(0, heads, summarize, 0)

    first_member = lax.div(me, group) * group
    mine = lax.rem(me, group)

    def member(k):
        return lax.rem(mine + k, group)

    def give_summary(k, carry):
        m = member(k)
        to_ctx(sum_send.at[m], sum_recv.at[mine], SUM, first_member + m).start()
        return carry

    lax.fori_loop(1, group, give_summary, 0)
    sum_recv[mine] = sum_send[mine]

    def query_side(h, carry):
        for b in range(blocks):
            g2 = halves(out_ref[h, b])
            weights = nt2(g2, v_bal[h, b]) * shared_ref[b]
            weight_ref[h, b] = weights
            dq = nn3(halves(weights), halves(kd_ref[h, b]))
            dq = dq + valid_ref[b] * nn3(g2, halves(state_ref[h, b]))
            dq_bal[h, b] = dq * eq_ref[h, b]
        return carry

    lax.fori_loop(0, heads, query_side, 0)

    def column_of(ref, h):
        return cat([ref[h, b].astype(BF) for b in range(blocks)], 0)

    halfway = (heads + 1) // 2
    for c in range(halfway):
        pair = [column_of(dq_bal, c)]
        if halfway + c < heads:
            pair.append(column_of(dq_bal, halfway + c))
        else:
            pair.append(jnp.zeros((rows, LANES), BF))
        sent = dot(back_ref[...], cat(pair, 1), NN)
        slab = cat(
            [sent[:, a * LANES : (a + 1) * LANES].reshape(count, cap, LANES) for a in range(2)],
            1,
        )
        dq_send[c] = slab.astype(BF)

    def home_queries(k, carry):
        d = peer(me, k, count)
        to_ctx(
            dq_send.at[pl.ds(0, halfway), d], dq_recv.at[pl.ds(0, halfway), me], DQ, d
        ).start()
        return carry

    wait_all(sum_recv.at[pl.ds(0, group - 1)], SUM)
    lax.fori_loop(1, count, home_queries, 0)
    for c in range(halfway):
        dq_recv[c, me] = dq_send[c, me]

    def scan(h, carry):
        total = jnp.zeros((part, LANES), F32)
        for m in reversed(range(group)):
            total = sum_recv[m, h] + sum_recv[m, heads, pl.ds(h, 1)] * total
        tot_send[h] = total
        return carry

    lax.fori_loop(0, heads, scan, 0)
    groups = count // group
    if groups > 1:
        to_ctx(tot_send, tot_recv, TOT, lax.rem(me + count - group, count)).start()

    def key_side(h, carry):
        for b in range(blocks):
            dk_bal[h, b] = ek_ref[h, b] * nn3(
                halves(weight_ref[h, b].T), halves(qd_ref[h, b])
            )
            dv_bal[h, b] = nn3(halves(score_ref[h, b].T), halves(out_ref[h, b]))
        return carry

    if groups > 1:
        wait_all(tot_recv, TOT)

    def carries(h, carry):
        if groups > 1:
            total = tot_recv[h] * jnp.where(first_member + group == count, 0.0, 1.0)
        else:
            total = jnp.zeros((part, LANES), F32)
        for m in reversed(range(group)):
            car_send[m, h] = total
            total = sum_recv[m, h] + sum_recv[m, heads, pl.ds(h, 1)] * total
        return carry

    lax.fori_loop(0, heads, carries, 0)

    def give_carry(k, carry):
        m = member(k)
        to_ctx(car_send.at[m], car_recv.at[mine], CAR, first_member + m).start()
        return carry

    lax.fori_loop(1, group, give_carry, 0)
    car_recv[mine] = car_send[mine]
    lax.fori_loop(0, heads, key_side, 0)
    wait_all(car_recv.at[pl.ds(0, group - 1)], CAR)

    def finish(h, carry):
        bound = bound_ref[pl.ds(h, 1)]
        incoming = car_recv[:, h].reshape(LANES, LANES)
        pairs = [None] * blocks
        for b in reversed(range(blocks)):
            incoming2 = halves(incoming)
            tail = tail_ref[h, b]
            store = store_ref[h, b]
            sig = sig_ref[h, b]
            dv = dv_bal[h, b] + nt3(halves(store * tail), incoming2)
            dk = dk_bal[h, b] + tail * exact_nn2(v_bal[h, b], incoming2)
            mixture = q_bal[h, b].astype(F32) * dq_bal[h, b] - store * dk
            reach = shared_t_ref[b].astype(BF)
            slope = dot(cat([reach, reach, reach], 1), cat(thirds(mixture), 0), NN)
            slope = slope + last_ref[b] * jnp.sum(
                incoming * state_ref[h, b + 1], axis=0, keepdims=True
            )
            dp = (slope / forget_ref[h, b] - dk) * (1.0 - bound) * sig * (1.0 - sig)
            pairs[b] = cat([dv.astype(BF), dp.astype(BF)], 1)
            if b:
                incoming = back_state_ref[h, b] + factor_ref[h, b] * incoming
        sent = dot(back_ref[...], cat(pairs, 0), NN)
        slab = cat(
            [sent[:, a * LANES : (a + 1) * LANES].reshape(count, cap, LANES) for a in range(2)],
            1,
        )
        dvp_send[h] = slab.astype(BF)
        dvp_recv[h, me] = dvp_send[h, me]
        return carry

    for number, (first, past) in enumerate(chunks):
        lax.fori_loop(first, past, finish, 0)

        def home(k, carry):
            d = peer(me, k, count)
            span = pl.ds(first, past - first)
            to_ctx(dvp_send.at[span, d], dvp_recv.at[span, me], DVP + number, d).start()
            return carry

        lax.fori_loop(1, count, home, 0)

    wait_all(dq_recv.at[pl.ds(0, halfway), pl.ds(0, count - 1)], DQ)
    for c in range(halfway):
        rows_home = dot(settle_ref[...], unslab(dq_recv[c], 2), NN).astype(BF)
        for a in range(2):
            h = c + a * halfway
            if h < heads:
                dq_ref[:, h * LANES : (h + 1) * LANES] = rows_home[:, a * LANES : (a + 1) * LANES]

    def settle(h, carry):
        rows_home = dot(settle_ref[...], unslab(dvp_recv[h], 2), NN).astype(BF)
        at = pl.ds(pl.multiple_of(h * LANES, LANES), LANES)
        dv_ref[:, at] = rows_home[:, :LANES]
        dp_ref[:, at] = rows_home[:, LANES:]
        return carry

    for number, (first, past) in enumerate(chunks):
        span = pl.ds(first, past - first)
        wait_all(dvp_recv.at[span, pl.ds(0, count - 1)], DVP + number)
        lax.fori_loop(first, past, settle, 0)

    drain(req_send.at[pl.ds(0, count - 1)], send_sem, REQ)
    if head_count > 1:
        drain(stat_recv.at[pl.ds(0, head_count - 1)], send_sem, STAT)
    drain(sum_send.at[pl.ds(0, group - 1)], send_sem, SUM)
    if groups > 1:
        drain(tot_send, send_sem, TOT)
    drain(car_send.at[pl.ds(0, group - 1)], send_sem, CAR)
    drain(dq_send.at[pl.ds(0, halfway), pl.ds(0, count - 1)], send_sem, DQ)
    for number, (first, past) in enumerate(chunks):
        span = pl.ds(first, past - first)
        drain(row_send.at[span, pl.ds(0, count - 1)], send_sem, ROWS + number)
        drain(dvp_send.at[span, pl.ds(0, count - 1)], send_sem, DVP + number)


def body(
    count,
    head_count,
    query_rows,
    gate_rows,
    value_rows,
    upstream_rows,
    row_map,
    doc_lengths,
    entry_state,
    lower_bound,
    norm_gain,
):
    rows = row_map.shape[0]
    heads = entry_state.shape[1]
    cap = 2 * rows // count
    slots = count * cap
    blocks = rows // BLOCK
    group = DOC_MOST // rows
    chunks = tuple((h, h + 1) for h in range(heads))
    sizes = (count, head_count, rows, heads, cap, group, chunks)
    small = jnp.concatenate([row_map, doc_lengths])
    small = jnp.pad(small, (0, 8 * LANES - small.shape[0])).reshape(8, LANES)
    part = LANES // group
    halfway = (heads + 1) // 2
    vmem = pltpu.VMEM
    per_block = (heads, blocks, BLOCK, LANES)
    semaphores = 6 + 2 * len(chunks)
    scratch = [
        vmem((count, cap, LANES), F32),
        vmem((count, cap, LANES), F32),
        vmem((heads, count, 4 * cap, LANES), BF),
        vmem((heads, count, 4 * cap, LANES), BF),
        vmem((halfway, count, 2 * cap, LANES), BF),
        vmem((halfway, count, 2 * cap, LANES), BF),
        vmem((heads, count, 2 * cap, LANES), BF),
        vmem((heads, count, 2 * cap, LANES), BF),
        vmem((group, heads + 1, part, LANES), F32),
        vmem((group, heads + 1, part, LANES), F32),
        vmem((heads, part, LANES), F32),
        vmem((heads, part, LANES), F32),
        vmem((group, heads, part, LANES), F32),
        vmem((group, heads, part, LANES), F32),
        vmem((8, rows), F32),
        vmem((head_count, 8, rows), F32),
        vmem((slots, rows), BF),
        vmem((rows, slots), BF),
        vmem((rows, slots), BF),
        vmem((slots, rows), BF),
        vmem((blocks, BLOCK, BLOCK), F32),
        vmem((blocks, BLOCK, BLOCK), F32),
        vmem((blocks, BLOCK, LANES), F32),
        vmem((blocks, BLOCK, LANES), F32),
        vmem((blocks, LANES), F32),
        vmem(per_block, BF),
        vmem(per_block, BF),
        vmem(per_block, BF),
        vmem(per_block, F32),
        vmem(per_block, F32),
        vmem(per_block, F32),
        vmem(per_block, F32),
        vmem(per_block, F32),
        vmem(per_block, F32),
        vmem(per_block, F32),
        vmem(per_block, F32),
        vmem(per_block, F32),
        vmem(per_block, F32),
        vmem((heads, blocks + 1, LANES, LANES), F32),
        vmem((heads, blocks, 1, LANES), F32),
        vmem((heads, blocks, LANES, LANES), F32),
        vmem(per_block, F32),
        vmem(per_block, F32),
        vmem(per_block, F32),
        vmem(per_block, F32),
        vmem((rows, LANES), F32),
        vmem((rows, LANES), F32),
        pltpu.SemaphoreType.DMA((semaphores,)),
        pltpu.SemaphoreType.DMA((semaphores,)),
    ]
    whole = pl.BlockSpec(memory_space=pltpu.VMEM)
    shape = jax.ShapeDtypeStruct(query_rows.shape, BF)
    return pl.pallas_call(
        functools.partial(kernel, sizes),
        out_shape=(shape, shape, shape),
        in_specs=[whole] * 8,
        out_specs=(whole, whole, whole),
        scratch_shapes=scratch,
        compiler_params=pltpu.CompilerParams(
            collective_id=0, has_side_effects=True, vmem_limit_bytes=56 << 20
        ),
    )(
        small,
        query_rows,
        gate_rows,
        value_rows,
        upstream_rows,
        entry_state,
        lower_bound.reshape(heads, LANES),
        norm_gain.reshape(heads, LANES),
    )


def solution(mesh):
    placed = (
        P("ctx", "head"),
        P("ctx", "head"),
        P("ctx", "head"),
        P("ctx", "head"),
        P("ctx"),
        P(),
        P("ctx", "head", None, None),
        P("head"),
        P("head"),
    )
    return jax.shard_map(
        functools.partial(body, mesh.shape["ctx"], mesh.shape["head"]),
        mesh=mesh,
        in_specs=placed,
        out_specs=(P("ctx", "head"), P("ctx", "head"), P("ctx", "head")),
        check_vma=False,
    )
```

```python
import functools

import jax
import jax.numpy as jnp
from jax import lax
from jax.experimental import pallas as pl
from jax.experimental.pallas import tpu as pltpu
from jax.sharding import PartitionSpec as P

BLOCK = 128
LANES = 128
DOC_MOST = 2048
EPSILON = 1e-06
MESH = pl.DeviceIdType.MESH
BF = jnp.bfloat16
F32 = jnp.float32
NN = (((1,), (0,)), ((), ()))
NT = (((1,), (1,)), ((), ()))


def dot(a, b, dims):
    return lax.dot_general(a, b, dims, preferred_element_type=F32)


def cat(parts, axis):
    return jnp.concatenate(parts, axis=axis)


def halves(x):
    high = x.astype(BF)
    return high, (x - high.astype(F32)).astype(BF)


def thirds(x):
    high = x.astype(BF)
    rest = x - high.astype(F32)
    middle = rest.astype(BF)
    return high, middle, (rest - middle.astype(F32)).astype(BF)


def nn3(a, b):
    return dot(cat([a[0], a[0], a[1]], 1), cat([b[0], b[1], b[0]], 0), NN)


def nt3(a, b):
    return dot(cat([a[0], a[0], a[1]], 1), cat([b[0], b[1], b[0]], 1), NT)


def nn2(a, exact):
    return dot(cat(a, 1), cat([exact, exact], 0), NN)


def nt2(a, exact):
    return dot(cat(a, 1), cat([exact, exact], 1), NT)


def exact_nn2(exact, b):
    return dot(cat([exact, exact], 1), cat(b, 0), NN)


def iota(shape, axis):
    return lax.broadcasted_iota(jnp.int32, shape, axis)


def one(mask):
    return jnp.where(mask, 1.0, 0.0).astype(F32)


def column(row):
    parts = [
        jnp.broadcast_to(row[:, at : at + LANES], (LANES, LANES)).T
        for at in range(0, row.shape[1], LANES)
    ]
    return cat(parts, 0) if len(parts) > 1 else parts[0]


def widen(col, width):
    return cat([col] * (width // LANES), 1)


def spread(me, count, start):
    if count != 64:

        def one_of(k, carry):
            start(lax.rem(me + k, count))
            return carry

        lax.fori_loop(1, count, one_of, 0)
        return
    y, w = lax.div(me, 8), lax.rem(me, 8)

    def along_y(w_there, first):
        for dy in range(first, 8):
            start(lax.rem(y + dy, 8) * 8 + w_there)

    def across(dw, carry):
        along_y(lax.rem(w + dw, 8), 0)
        return carry

    along_y(w, 1)
    lax.fori_loop(1, 8, across, 0)


def kernel(
    sizes,
    map_ref,
    length_ref,
    q_ref,
    p_ref,
    v_ref,
    y_ref,
    entry_ref,
    bound_ref,
    gain_ref,
    grad_ref,
    req_send,
    req_recv,
    row_send,
    row_recv,
    dq_send,
    dq_recv,
    dvp_send,
    dvp_recv,
    sum_send,
    sum_recv,
    tot_send,
    tot_recv,
    car_send,
    car_recv,
    stat_send,
    stat_recv,
    gather_ref,
    settle_ref,
    place_ref,
    back_ref,
    shared_ref,
    shared_t_ref,
    valid_ref,
    last_ref,
    through_ref,
    q_bal,
    v_bal,
    y_bal,
    sig_ref,
    forget_ref,
    store_ref,
    ek_ref,
    tail_ref,
    qd_ref,
    score_t_ref,
    up_t_ref,
    out_t_ref,
    up_weight_ref,
    out_weight_ref,
    up_query_ref,
    out_query_ref,
    scale_ref,
    state_ref,
    factor_ref,
    back_state_ref,
    out_ref,
    dq_bal,
    dk_bal,
    dv_bal,
    square_ref,
    cross_ref,
    send_sem,
    recv_sem,
):
    count, head_count, rows, heads, cap, group, chunks = sizes
    slots = count * cap
    blocks = rows // BLOCK
    part = LANES // group
    me = lax.axis_index("ctx")
    plane = lax.axis_index("head")
    base = me * rows

    def to_ctx(src, dst, sem, d):
        return pltpu.make_async_remote_copy(
            src_ref=src,
            dst_ref=dst,
            send_sem=send_sem.at[sem],
            recv_sem=recv_sem.at[sem],
            device_id={"ctx": d},
            device_id_type=MESH,
        )

    def drain(view, sems, sem):
        pltpu.make_async_copy(view, view, sems.at[sem]).wait()

    leaving, due = [], []

    def note(sending, receiving, sem):
        leaving.append((sending, sem))
        due.append((receiving, sem))

    def arrive():
        view, sem = due.pop(0)
        drain(view, recv_sem, sem)

    REQ, STAT, SUM, TOT, CAR, DQ, ROWS = 0, 1, 2, 3, 4, 5, 8
    DVP = ROWS + len(chunks)

    barrier = pltpu.get_barrier_semaphore()

    def greet_plane(k, carry):
        pl.semaphore_signal(
            barrier,
            inc=1,
            device_id={"head": lax.rem(plane + k, head_count)},
            device_id_type=MESH,
        )
        return carry

    spread(
        me,
        count,
        lambda d: pl.semaphore_signal(
            barrier, inc=1, device_id={"ctx": d}, device_id_type=MESH
        ),
    )
    lax.fori_loop(1, head_count, greet_plane, 0)

    map_row = cat([map_ref[b : b + 1] for b in range(blocks)], 1).astype(F32)
    source_row = jnp.floor(map_row * (1.0 / rows))
    local_col = column(map_row - source_row * rows)
    source_col = column(source_row)
    same = (widen(source_col, rows) == source_row) & (
        iota((rows, rows), 0) < iota((rows, rows), 1)
    )
    rank_row = jnp.sum(one(same), axis=0, keepdims=True)
    slot_row = source_row * cap + rank_row
    back_ref[...] = one(iota((slots, rows), 0).astype(F32) == slot_row).astype(BF)
    asked_mine = dot(back_ref[...], (local_col + 1.0).astype(BF), NN)
    own_lane = iota((count, cap, LANES), 1) == iota((count, cap, LANES), 2)
    req_send[...] = jnp.sum(
        jnp.where(own_lane, asked_mine.reshape(count, cap, LANES), 0.0), axis=1, keepdims=True
    )

    pl.semaphore_wait(barrier, count - 1 + head_count - 1)
    others = pl.ds(0, count - 1)
    spread(
        me, count, lambda d: to_ctx(req_send.at[d], req_recv.at[me], REQ, d).start()
    )
    note(req_send.at[others], req_recv.at[others], REQ)
    req_recv[me] = req_send[me]

    place_ref[...] = one(
        iota((rows, slots), 1).astype(F32) == widen(column(slot_row), slots)
    ).astype(BF)

    lengths = length_ref[...].astype(F32)
    length_col = column(cat([lengths, jnp.zeros((1, LANES - lengths.shape[1]), F32)], 1))
    ends_row = jnp.sum(
        jnp.where(iota((LANES, LANES), 0) <= iota((LANES, LANES), 1), length_col, 0.0),
        axis=0,
        keepdims=True,
    )
    ends_col = column(ends_row)
    position = (iota((1, rows), 1) + base).astype(F32)
    document_row = jnp.sum(one(widen(ends_col, rows) <= position), axis=0, keepdims=True)
    document_col = column(document_row)
    before = (iota((1, LANES), 1) * 0 + (base - 1)).astype(F32)
    before = jnp.where(
        before < 0.0, -1.0, jnp.sum(one(ends_col <= before), axis=0, keepdims=True)
    )
    for b in range(blocks):
        at = slice(b * BLOCK, (b + 1) * BLOCK)
        previous = before if b == 0 else document_col[b * BLOCK - 1 : b * BLOCK]
        final = document_col[(b + 1) * BLOCK - 1 : (b + 1) * BLOCK]
        alike = document_col[at] == document_row[:, at]
        earlier = iota((BLOCK, BLOCK), 0) >= iota((BLOCK, BLOCK), 1)
        later = iota((BLOCK, BLOCK), 0) <= iota((BLOCK, BLOCK), 1)
        shared_ref[b] = one(alike & earlier)
        shared_t_ref[b] = one(alike & later)
        valid_ref[b] = one(document_col[at] == previous)
        last_ref[b] = one(document_col[at] == final)
        through_ref[pl.ds(b, 1)] = one(previous == final)

    arrive()
    asked = jnp.broadcast_to(req_recv[...], (count, cap, LANES))
    asked = jnp.where(own_lane, asked, 0.0).reshape(slots, LANES).astype(BF)
    asked = dot(asked, jnp.ones((LANES, LANES), BF), NN)
    gather = cat(
        [
            one(asked == (iota((slots, LANES), 1) + (b * LANES + 1)).astype(F32))
            for b in range(blocks)
        ],
        1,
    )
    gather_ref[...] = gather.astype(BF)

    step_slots = min(slots, 128)
    step_peers = step_slots // cap
    for number, (first, past) in enumerate(chunks):

        def pack(h, carry):
            at = pl.ds(pl.multiple_of(h * LANES, LANES), LANES)
            wide = cat([q_ref[:, at], p_ref[:, at], v_ref[:, at], y_ref[:, at]], 1)
            for piece in range(slots // step_slots):
                picked = dot(
                    gather_ref[piece * step_slots : (piece + 1) * step_slots], wide, NN
                )
                slab = cat(
                    [
                        picked[:, a * LANES : (a + 1) * LANES].reshape(step_peers, cap, LANES)
                        for a in range(4)
                    ],
                    1,
                )
                row_send[h, piece * step_peers : (piece + 1) * step_peers] = slab.astype(BF)
            return carry

        lax.fori_loop(first, past, pack, 0)

        span = pl.ds(first, past - first)
        spread(
            me,
            count,
            lambda d: to_ctx(
                row_send.at[span, d], row_recv.at[span, me], ROWS + number, d
            ).start(),
        )
        note(row_send.at[span, others], row_recv.at[span, others], ROWS + number)

    def own(h, carry):
        row_recv[h, me] = row_send[h, me]
        return carry

    lax.fori_loop(0, heads, own, 0)
    settle_ref[...] = gather.T.astype(BF)

    square_ref[...] = jnp.zeros_like(square_ref)
    cross_ref[...] = jnp.zeros_like(cross_ref)
    lower = one(iota((BLOCK, BLOCK), 0) >= iota((BLOCK, BLOCK), 1)).astype(BF)
    lower3 = cat([lower, lower, lower], 1)

    def unslab(slab, parts):
        wide = slab.astype(F32)
        return cat(
            [
                wide[:, a * cap : (a + 1) * cap].reshape(slots, LANES).astype(BF)
                for a in range(parts)
            ],
            1,
        )

    def forward(h, carry):
        balanced = dot(place_ref[...], unslab(row_recv[h], 4), NN)
        bound = bound_ref[pl.ds(h, 1)]
        gain = gain_ref[pl.ds(h, 1)]
        state = entry_ref[0, h].T
        for b in range(blocks):
            at = slice(b * BLOCK, (b + 1) * BLOCK)
            q, p, v, y = [balanced[at, a * LANES : (a + 1) * LANES] for a in range(4)]
            v_exact = v.astype(BF)
            sig = jax.nn.sigmoid(p)
            forget = bound + (1.0 - bound) * sig
            store = 1.0 - forget
            decay = dot(lower3, cat(thirds(jnp.log(forget)), 0), NN)
            total = decay[BLOCK - 1 : BLOCK]
            eq = jnp.exp(decay)
            ek = jnp.exp(-decay)
            tail = jnp.exp(total - decay) * last_ref[b]
            factor = through_ref[pl.ds(b, 1)] * jnp.exp(total)
            qd = q * eq
            kd = store * ek
            qd2 = halves(qd)
            kd2 = halves(kd)
            state2 = halves(state)
            scores = nt3(qd2, kd2) * shared_ref[b]
            out = nn2(halves(scores), v_exact) + valid_ref[b] * nt3(qd2, state2)
            up = gain * y
            square_ref[at] += out * out
            cross_ref[at] += up * out
            state_ref[h, b] = state
            state = state * factor + exact_nn2(v.T.astype(BF), halves(store * tail))
            for value, weight_ref, query_ref, turned_ref in (
                (up, up_weight_ref, up_query_ref, up_t_ref),
                (out, out_weight_ref, out_query_ref, out_t_ref),
            ):
                value2 = halves(value)
                weights = nt2(value2, v_exact) * shared_ref[b]
                query_ref[h, b] = eq * (
                    nn3(halves(weights), kd2) + valid_ref[b] * nn3(value2, state2)
                )
                weight_ref[h, b] = weights.T
                turned_ref[h, b] = (value * valid_ref[b]).T
            q_bal[h, b] = q.astype(BF)
            v_bal[h, b] = v_exact
            y_bal[h, b] = y.astype(BF)
            sig_ref[h, b] = sig
            forget_ref[h, b] = forget
            store_ref[h, b] = store
            ek_ref[h, b] = ek
            tail_ref[h, b] = tail
            qd_ref[h, b, 0], qd_ref[h, b, 1] = qd2
            score_t_ref[h, b, 0], score_t_ref[h, b, 1] = halves(scores.T)
            factor_ref[h, b] = factor
            out_ref[h, b] = out
        state_ref[h, blocks] = state
        return carry

    for number, (first, past) in enumerate(chunks):
        if number + 1 == len(chunks):
            pass
        arrive()
        if number + 1 == len(chunks):
            pass
        lax.fori_loop(first, past, forward, 0)

    ones = jnp.ones((8, 3 * LANES), BF)
    squares = dot(ones, cat(thirds(square_ref[...]), 1), NT)
    crosses = dot(ones, cat(thirds(cross_ref[...]), 1), NT)
    stat_send[...] = jnp.where(iota((8, rows), 0) < 4, squares, crosses)

    def share(k, carry):
        pltpu.make_async_remote_copy(
            src_ref=stat_send,
            dst_ref=stat_recv.at[plane],
            send_sem=send_sem.at[STAT],
            recv_sem=recv_sem.at[STAT],
            device_id={"head": lax.rem(plane + k, head_count)},
            device_id_type=MESH,
        ).start()
        return carry

    lax.fori_loop(1, head_count, share, 0)
    if head_count > 1:
        planes = stat_recv.at[pl.ds(0, head_count - 1)]
        note(planes, planes, STAT)
    stat_recv[plane] = stat_send[...]
    sum_send[...] = jnp.zeros_like(sum_send)
    if head_count > 1:
        arrive()
    stats = jnp.sum(stat_recv[...], axis=0)
    width = float(head_count * heads * LANES)
    inverse = lax.rsqrt(stats[0:1] / width + EPSILON)
    slope = inverse * inverse * inverse * (stats[4:5] / width)
    square_ref[...] = column(inverse)
    cross_ref[...] = column(slope)
    scale_ref[0:1] = inverse
    scale_ref[1:2] = slope

    def pair(ref, h, b):
        return ref[h, b, 0], ref[h, b, 1]

    def mixed_t(up_part, out_part, b):
        at = slice(b * BLOCK, (b + 1) * BLOCK)
        return scale_ref[0:1, at] * up_part - scale_ref[1:2, at] * out_part

    def summarize(h, carry):
        back = []
        for b in range(blocks):
            turned = mixed_t(up_t_ref[h, b], out_t_ref[h, b], b)
            back.append(nn3(halves(turned), pair(qd_ref, h, b)))
            back_state_ref[h, b] = back[b]
        summary = back[blocks - 1]
        decay = factor_ref[h, blocks - 1]
        for b in reversed(range(blocks - 1)):
            summary = back[b] + factor_ref[h, b] * summary
            decay = decay * factor_ref[h, b]
        sum_send[:, h] = summary.reshape(group, part, LANES)
        sum_send[:, heads, pl.ds(h, 1)] = jnp.broadcast_to(decay[None], (group, 1, LANES))
        return carry

    lax.fori_loop(0, heads, summarize, 0)

    first_member = lax.div(me, group) * group
    mine = lax.rem(me, group)

    def member(k):
        return lax.rem(mine + k, group)

    def give_summary(k, carry):
        m = member(k)
        to_ctx(sum_send.at[m], sum_recv.at[mine], SUM, first_member + m).start()
        return carry

    lax.fori_loop(1, group, give_summary, 0)
    members = pl.ds(0, group - 1)
    note(sum_send.at[members], sum_recv.at[members], SUM)
    sum_recv[mine] = sum_send[mine]

    def query_part(first, past, sem):
        def query_side(h, carry):
            parts = []
            for b in range(blocks):
                at = slice(b * BLOCK, (b + 1) * BLOCK)
                dq = square_ref[at] * up_query_ref[h, b] - cross_ref[at] * out_query_ref[h, b]
                dq_bal[h, b] = dq
                parts.append(dq.astype(BF))
            away = dot(back_ref[...], cat(parts, 0), NN)
            dq_send[h] = away.reshape(count, cap, LANES).astype(BF)
            dq_recv[h, me] = dq_send[h, me]
            return carry

        lax.fori_loop(first, past, query_side, 0)
        span = pl.ds(first, past - first)
        spread(
            me,
            count,
            lambda d: to_ctx(dq_send.at[span, d], dq_recv.at[span, me], sem, d).start(),
        )
        leaving.append((dq_send.at[span, others], sem))
        return dq_recv.at[span, others], sem

    cuts = [heads * i // 3 for i in range(4)]
    dq_due = [query_part(cuts[0], cuts[1], DQ)]

    arrive()

    def scan(h, carry):
        total = jnp.zeros((part, LANES), F32)
        for m in reversed(range(group)):
            total = sum_recv[m, h] + sum_recv[m, heads, pl.ds(h, 1)] * total
        tot_send[h] = total
        return carry

    lax.fori_loop(0, heads, scan, 0)
    groups = count // group
    if groups > 1:
        to_ctx(tot_send, tot_recv, TOT, lax.rem(me + count - group, count)).start()
        note(tot_send, tot_recv, TOT)
    dq_due.append(query_part(cuts[1], cuts[2], DQ + 1))

    if groups > 1:
        arrive()

    def carries(h, carry):
        if groups > 1:
            total = tot_recv[h] * jnp.where(first_member + group == count, 0.0, 1.0)
        else:
            total = jnp.zeros((part, LANES), F32)
        for m in reversed(range(group)):
            car_send[m, h] = total
            total = sum_recv[m, h] + sum_recv[m, heads, pl.ds(h, 1)] * total
        return carry

    lax.fori_loop(0, heads, carries, 0)

    def give_carry(k, carry):
        m = member(k)
        to_ctx(car_send.at[m], car_recv.at[mine], CAR, first_member + m).start()
        return carry

    lax.fori_loop(1, group, give_carry, 0)
    note(car_send.at[members], car_recv.at[members], CAR)
    car_recv[mine] = car_send[mine]
    dq_due.append(query_part(cuts[2], cuts[3], DQ + 2))

    def key_side(h, carry):
        gain = gain_ref[pl.ds(h, 1)]
        for b in range(blocks):
            at = slice(b * BLOCK, (b + 1) * BLOCK)
            g = square_ref[at] * (gain * y_bal[h, b].astype(F32)) - cross_ref[at] * out_ref[h, b]
            weights = mixed_t(up_weight_ref[h, b], out_weight_ref[h, b], b)
            dk_bal[h, b] = ek_ref[h, b] * nn3(halves(weights), pair(qd_ref, h, b))
            dv_bal[h, b] = nn3(pair(score_t_ref, h, b), halves(g))
        return carry

    lax.fori_loop(0, heads, key_side, 0)
    arrive()
    due.extend(dq_due)

    def finish(h, carry):
        bound = bound_ref[pl.ds(h, 1)]
        incoming = car_recv[:, h].reshape(LANES, LANES)
        pairs = [None] * blocks
        for b in reversed(range(blocks)):
            incoming2 = halves(incoming)
            tail = tail_ref[h, b]
            store = store_ref[h, b]
            sig = sig_ref[h, b]
            dv = dv_bal[h, b] + nt3(halves(store * tail), incoming2)
            dk = dk_bal[h, b] + tail * exact_nn2(v_bal[h, b], incoming2)
            mixture = q_bal[h, b].astype(F32) * dq_bal[h, b] - store * dk
            reach = shared_t_ref[b].astype(BF)
            slope = dot(cat([reach, reach, reach], 1), cat(thirds(mixture), 0), NN)
            slope = slope + last_ref[b] * jnp.sum(
                incoming * state_ref[h, b + 1], axis=0, keepdims=True
            )
            dp = (slope / forget_ref[h, b] - dk) * (1.0 - bound) * sig * (1.0 - sig)
            pairs[b] = cat([dv.astype(BF), dp.astype(BF)], 1)
            if b:
                incoming = back_state_ref[h, b] + factor_ref[h, b] * incoming
        away = dot(back_ref[...], cat(pairs, 0), NN)
        slab = cat(
            [away[:, a * LANES : (a + 1) * LANES].reshape(count, cap, LANES) for a in range(2)],
            1,
        )
        dvp_send[h] = slab.astype(BF)
        dvp_recv[h, me] = dvp_send[h, me]
        return carry

    for number, (first, past) in enumerate(chunks):
        lax.fori_loop(first, past, finish, 0)

        span = pl.ds(first, past - first)
        spread(
            me,
            count,
            lambda d: to_ctx(
                dvp_send.at[span, d], dvp_recv.at[span, me], DVP + number, d
            ).start(),
        )
        note(dvp_send.at[span, others], dvp_recv.at[span, others], DVP + number)

    def settle_query(h, carry):
        slab = dq_recv[h].astype(F32).reshape(slots, LANES).astype(BF)
        at = pl.ds(pl.multiple_of(h * LANES, LANES), LANES)
        grad_ref[0, :, at] = dot(settle_ref[...], slab, NN).astype(BF)
        return carry

    for first, past in zip(cuts[:-1], cuts[1:]):
        arrive()
        lax.fori_loop(first, past, settle_query, 0)

    def settle(h, carry):
        rows_home = dot(settle_ref[...], unslab(dvp_recv[h], 2), NN).astype(BF)
        at = pl.ds(pl.multiple_of(h * LANES, LANES), LANES)
        grad_ref[2, :, at] = rows_home[:, :LANES]
        grad_ref[1, :, at] = rows_home[:, LANES:]
        return carry

    for number, (first, past) in enumerate(chunks):
        if number + 1 == len(chunks):
            pass
        arrive()
        if number + 1 == len(chunks):
            pass
        lax.fori_loop(first, past, settle, 0)

    for view, sem in leaving:
        drain(view, send_sem, sem)


def unstack(grad_ref, dq_ref, dp_ref, dv_ref):
    dq_ref[...] = grad_ref[0]
    dp_ref[...] = grad_ref[1]
    dv_ref[...] = grad_ref[2]


def body(
    count,
    head_count,
    query_rows,
    gate_rows,
    value_rows,
    upstream_rows,
    row_map,
    doc_lengths,
    entry_state,
    lower_bound,
    norm_gain,
):
    rows = row_map.shape[0]
    heads = entry_state.shape[1]
    cap = 2 * rows // count
    slots = count * cap
    blocks = rows // BLOCK
    group = DOC_MOST // rows
    chunks = tuple((h, h + 1) for h in range(heads))
    sizes = (count, head_count, rows, heads, cap, group, chunks)
    part = LANES // group
    vmem = pltpu.VMEM
    per_block = (heads, blocks, BLOCK, LANES)
    split_block = (heads, blocks, 2, BLOCK, LANES)
    semaphores = 8 + 2 * len(chunks)
    scratch = [
        vmem((count, 1, LANES), F32),
        vmem((count, 1, LANES), F32),
        vmem((heads, count, 4 * cap, LANES), BF),
        vmem((heads, count, 4 * cap, LANES), BF),
        vmem((heads, count, cap, LANES), BF),
        vmem((heads, count, cap, LANES), BF),
        vmem((heads, count, 2 * cap, LANES), BF),
        vmem((heads, count, 2 * cap, LANES), BF),
        vmem((group, heads + 1, part, LANES), F32),
        vmem((group, heads + 1, part, LANES), F32),
        vmem((heads, part, LANES), F32),
        vmem((heads, part, LANES), F32),
        vmem((group, heads, part, LANES), F32),
        vmem((group, heads, part, LANES), F32),
        vmem((8, rows), F32),
        vmem((head_count, 8, rows), F32),
        vmem((slots, rows), BF),
        vmem((rows, slots), BF),
        vmem((rows, slots), BF),
        vmem((slots, rows), BF),
        vmem((blocks, BLOCK, BLOCK), F32),
        vmem((blocks, BLOCK, BLOCK), F32),
        vmem((blocks, BLOCK, LANES), F32),
        vmem((blocks, BLOCK, LANES), F32),
        vmem((blocks, LANES), F32),
        vmem(per_block, BF),
        vmem(per_block, BF),
        vmem(per_block, BF),
        vmem(per_block, F32),
        vmem(per_block, F32),
        vmem(per_block, F32),
        vmem(per_block, F32),
        vmem(per_block, F32),
        vmem(split_block, BF),
        vmem(split_block, BF),
        vmem(per_block, F32),
        vmem(per_block, F32),
        vmem(per_block, F32),
        vmem(per_block, F32),
        vmem(per_block, F32),
        vmem(per_block, F32),
        vmem((2, rows), F32),
        vmem((heads, blocks + 1, LANES, LANES), F32),
        vmem((heads, blocks, 1, LANES), F32),
        vmem((heads, blocks, LANES, LANES), F32),
        vmem(per_block, F32),
        vmem(per_block, F32),
        vmem(per_block, F32),
        vmem(per_block, F32),
        vmem((rows, LANES), F32),
        vmem((rows, LANES), F32),
        pltpu.SemaphoreType.DMA((semaphores,)),
        pltpu.SemaphoreType.DMA((semaphores,)),
    ]
    whole = pl.BlockSpec(memory_space=pltpu.VMEM)
    shape = jax.ShapeDtypeStruct(query_rows.shape, BF)
    grads = pl.pallas_call(
        functools.partial(kernel, sizes),
        out_shape=jax.ShapeDtypeStruct((3,) + query_rows.shape, BF),
        in_specs=[whole] * 9,
        out_specs=whole,
        scratch_shapes=scratch,
        compiler_params=pltpu.CompilerParams(
            collective_id=0, has_side_effects=True, vmem_limit_bytes=56 << 20
        ),
    )(
        row_map.reshape(blocks, LANES),
        doc_lengths.reshape(1, doc_lengths.shape[0]),
        query_rows,
        gate_rows,
        value_rows,
        upstream_rows,
        entry_state,
        lower_bound.reshape(heads, LANES),
        norm_gain.reshape(heads, LANES),
    )
    return pl.pallas_call(
        unstack, out_shape=(shape, shape, shape), in_specs=[whole], out_specs=(whole,) * 3
    )(grads)


def solution(mesh):
    placed = (
        P("ctx", "head"),
        P("ctx", "head"),
        P("ctx", "head"),
        P("ctx", "head"),
        P("ctx"),
        P(),
        P("ctx", "head", None, None),
        P("head"),
        P("head"),
    )
    return jax.shard_map(
        functools.partial(body, mesh.shape["ctx"], mesh.shape["head"]),
        mesh=mesh,
        in_specs=placed,
        out_specs=(P("ctx", "head"), P("ctx", "head"), P("ctx", "head")),
        check_vma=False,
    )
```

```python
import functools

import jax
import jax.numpy as jnp
from jax import lax
from jax.experimental import pallas as pl
from jax.experimental.pallas import tpu as pltpu
from jax.sharding import PartitionSpec as P

BLOCK = 128
LANES = 128
DOC_MOST = 2048
EPSILON = 1e-06
MESH = pl.DeviceIdType.MESH
BF = jnp.bfloat16
F32 = jnp.float32
NN = (((1,), (0,)), ((), ()))
NT = (((1,), (1,)), ((), ()))


def dot(a, b, dims):
    return lax.dot_general(a, b, dims, preferred_element_type=F32)


def cat(parts, axis):
    return jnp.concatenate(parts, axis=axis)


def halves(x):
    high = x.astype(BF)
    return high, (x - high.astype(F32)).astype(BF)


def thirds(x):
    high = x.astype(BF)
    rest = x - high.astype(F32)
    middle = rest.astype(BF)
    return high, middle, (rest - middle.astype(F32)).astype(BF)


def nn3(a, b):
    return dot(cat([a[0], a[0], a[1]], 1), cat([b[0], b[1], b[0]], 0), NN)


def nt3(a, b):
    return dot(cat([a[0], a[0], a[1]], 1), cat([b[0], b[1], b[0]], 1), NT)


def nn2(a, exact):
    return dot(cat(a, 1), cat([exact, exact], 0), NN)


def nt2(a, exact):
    return dot(cat(a, 1), cat([exact, exact], 1), NT)


def exact_nn2(exact, b):
    return dot(cat([exact, exact], 1), cat(b, 0), NN)


def iota(shape, axis):
    return lax.broadcasted_iota(jnp.int32, shape, axis)


def one(mask):
    return jnp.where(mask, 1.0, 0.0).astype(F32)


def column(row):
    parts = [
        jnp.broadcast_to(row[:, at : at + LANES], (LANES, LANES)).T
        for at in range(0, row.shape[1], LANES)
    ]
    return cat(parts, 0) if len(parts) > 1 else parts[0]


def widen(col, width):
    return cat([col] * (width // LANES), 1)


def spread(me, count, start):
    if count != 64:

        def one_of(k, carry):
            start(lax.rem(me + k, count))
            return carry

        lax.fori_loop(1, count, one_of, 0)
        return
    y, w = lax.div(me, 8), lax.rem(me, 8)

    def along_y(w_there, first):
        for dy in range(first, 8):
            start(lax.rem(y + dy, 8) * 8 + w_there)

    def across(dw, carry):
        along_y(lax.rem(w + dw, 8), 0)
        return carry

    along_y(w, 1)
    lax.fori_loop(1, 8, across, 0)


def kernel(
    sizes,
    map_ref,
    length_ref,
    q_hbm,
    p_hbm,
    v_hbm,
    y_hbm,
    entry_hbm,
    bound_ref,
    gain_ref,
    grad_ref,
    q_ref,
    p_ref,
    v_ref,
    y_ref,
    entry_ref,
    load_sem,
    req_send,
    req_recv,
    row_send,
    row_recv,
    dq_send,
    dq_recv,
    dvp_send,
    dvp_recv,
    sum_send,
    sum_recv,
    tot_send,
    tot_recv,
    car_send,
    car_recv,
    stat_send,
    stat_recv,
    gather_ref,
    settle_ref,
    place_ref,
    back_ref,
    shared_ref,
    shared_t_ref,
    valid_ref,
    last_ref,
    through_ref,
    q_bal,
    v_bal,
    y_bal,
    sig_ref,
    forget_ref,
    store_ref,
    eq_ref,
    ek_ref,
    tail_ref,
    qd_ref,
    kd_ref,
    score_ref,
    score_t_ref,
    up_t_ref,
    out_t_ref,
    up_weight_ref,
    out_weight_ref,
    up_query_ref,
    out_query_ref,
    scale_ref,
    state_ref,
    factor_ref,
    back_state_ref,
    out_ref,
    dq_bal,
    dk_bal,
    dv_bal,
    square_ref,
    cross_ref,
    send_sem,
    recv_sem,
):
    count, head_count, rows, heads, cap, group, chunks = sizes
    slots = count * cap
    blocks = rows // BLOCK
    part = LANES // group
    me = lax.axis_index("ctx")
    plane = lax.axis_index("head")
    base = me * rows

    def to_ctx(src, dst, sem, d):
        return pltpu.make_async_remote_copy(
            src_ref=src,
            dst_ref=dst,
            send_sem=send_sem.at[sem],
            recv_sem=recv_sem.at[sem],
            device_id={"ctx": d},
            device_id_type=MESH,
        )

    def drain(view, sems, sem):
        pltpu.make_async_copy(view, view, sems.at[sem]).wait()

    leaving, due = [], []

    def note(sending, receiving, sem):
        leaving.append((sending, sem))
        due.append((receiving, sem))

    def arrive():
        view, sem = due.pop(0)
        drain(view, recv_sem, sem)

    REQ, STAT, SUM, TOT, CAR, DQ, ROWS = 0, 1, 2, 4, 6, 8, 11
    DVP = ROWS + len(chunks)

    barrier = pltpu.get_barrier_semaphore()

    def greet_plane(k, carry):
        pl.semaphore_signal(
            barrier,
            inc=1,
            device_id={"head": lax.rem(plane + k, head_count)},
            device_id_type=MESH,
        )
        return carry

    spread(
        me,
        count,
        lambda d: pl.semaphore_signal(
            barrier, inc=1, device_id={"ctx": d}, device_id_type=MESH
        ),
    )
    lax.fori_loop(1, head_count, greet_plane, 0)

    loads = [
        pltpu.make_async_copy(src, dst, load_sem.at[at])
        for at, (src, dst) in enumerate(
            (
                (q_hbm, q_ref),
                (p_hbm, p_ref),
                (v_hbm, v_ref),
                (y_hbm, y_ref),
                (entry_hbm, entry_ref),
            )
        )
    ]
    for load in loads:
        load.start()

    map_row = cat([map_ref[b : b + 1] for b in range(blocks)], 1).astype(F32)
    source_row = jnp.floor(map_row * (1.0 / rows))
    local_col = column(map_row - source_row * rows)
    source_col = column(source_row)
    same = (widen(source_col, rows) == source_row) & (
        iota((rows, rows), 0) < iota((rows, rows), 1)
    )
    rank_row = jnp.sum(one(same), axis=0, keepdims=True)
    slot_row = source_row * cap + rank_row
    back_ref[...] = one(iota((slots, rows), 0).astype(F32) == slot_row).astype(BF)
    asked_mine = dot(back_ref[...], (local_col + 1.0).astype(BF), NN)
    own_lane = iota((count, cap, LANES), 1) == iota((count, cap, LANES), 2)
    req_send[...] = jnp.sum(
        jnp.where(own_lane, asked_mine.reshape(count, cap, LANES), 0.0), axis=1, keepdims=True
    )

    pl.semaphore_wait(barrier, count - 1 + head_count - 1)
    others = pl.ds(0, count - 1)
    spread(
        me, count, lambda d: to_ctx(req_send.at[d], req_recv.at[me], REQ, d).start()
    )
    note(req_send.at[others], req_recv.at[others], REQ)
    req_recv[me] = req_send[me]

    place_ref[...] = one(
        iota((rows, slots), 1).astype(F32) == widen(column(slot_row), slots)
    ).astype(BF)

    lengths = length_ref[...].astype(F32)
    length_col = column(cat([lengths, jnp.zeros((1, LANES - lengths.shape[1]), F32)], 1))
    ends_row = jnp.sum(
        jnp.where(iota((LANES, LANES), 0) <= iota((LANES, LANES), 1), length_col, 0.0),
        axis=0,
        keepdims=True,
    )
    ends_col = column(ends_row)
    position = (iota((1, rows), 1) + base).astype(F32)
    document_row = jnp.sum(one(widen(ends_col, rows) <= position), axis=0, keepdims=True)
    document_col = column(document_row)
    before = (iota((1, LANES), 1) * 0 + (base - 1)).astype(F32)
    before = jnp.where(
        before < 0.0, -1.0, jnp.sum(one(ends_col <= before), axis=0, keepdims=True)
    )
    for b in range(blocks):
        at = slice(b * BLOCK, (b + 1) * BLOCK)
        previous = before if b == 0 else document_col[b * BLOCK - 1 : b * BLOCK]
        final = document_col[(b + 1) * BLOCK - 1 : (b + 1) * BLOCK]
        alike = document_col[at] == document_row[:, at]
        earlier = iota((BLOCK, BLOCK), 0) >= iota((BLOCK, BLOCK), 1)
        later = iota((BLOCK, BLOCK), 0) <= iota((BLOCK, BLOCK), 1)
        shared_ref[b] = one(alike & earlier)
        shared_t_ref[b] = one(alike & later)
        valid_ref[b] = one(document_col[at] == previous)
        last_ref[b] = one(document_col[at] == final)
        through_ref[pl.ds(b, 1)] = one(previous == final)

    for load in loads:
        load.wait()
    arrive()
    asked = jnp.broadcast_to(req_recv[...], (count, cap, LANES))
    asked = jnp.where(own_lane, asked, 0.0).reshape(slots, LANES).astype(BF)
    asked = dot(asked, jnp.ones((LANES, LANES), BF), NN)
    gather = cat(
        [
            one(asked == (iota((slots, LANES), 1) + (b * LANES + 1)).astype(F32))
            for b in range(blocks)
        ],
        1,
    )
    gather_ref[...] = gather.astype(BF)

    step_slots = min(slots, 128)
    step_peers = step_slots // cap
    for number, (first, past) in enumerate(chunks):

        def pack(h, carry):
            at = pl.ds(pl.multiple_of(h * LANES, LANES), LANES)
            wide = cat([q_ref[:, at], p_ref[:, at], v_ref[:, at], y_ref[:, at]], 1)
            for piece in range(slots // step_slots):
                picked = dot(
                    gather_ref[piece * step_slots : (piece + 1) * step_slots], wide, NN
                )
                slab = cat(
                    [
                        picked[:, a * LANES : (a + 1) * LANES].reshape(step_peers, cap, LANES)
                        for a in range(4)
                    ],
                    1,
                )
                row_send[h, piece * step_peers : (piece + 1) * step_peers] = slab.astype(BF)
            return carry

        lax.fori_loop(first, past, pack, 0)

        span = pl.ds(first, past - first)
        spread(
            me,
            count,
            lambda d: to_ctx(
                row_send.at[span, d], row_recv.at[span, me], ROWS + number, d
            ).start(),
        )
        note(row_send.at[span, others], row_recv.at[span, others], ROWS + number)

    def own(h, carry):
        row_recv[h, me] = row_send[h, me]
        return carry

    lax.fori_loop(0, heads, own, 0)
    settle_ref[...] = gather.T.astype(BF)

    square_ref[...] = jnp.zeros_like(square_ref)
    cross_ref[...] = jnp.zeros_like(cross_ref)
    lower = one(iota((BLOCK, BLOCK), 0) >= iota((BLOCK, BLOCK), 1)).astype(BF)
    lower3 = cat([lower, lower, lower], 1)

    def unslab(slab, parts):
        wide = slab.astype(F32)
        return cat(
            [
                wide[:, a * cap : (a + 1) * cap].reshape(slots, LANES).astype(BF)
                for a in range(parts)
            ],
            1,
        )

    def forward(h, carry):
        balanced = dot(place_ref[...], unslab(row_recv[h], 4), NN)
        bound = bound_ref[pl.ds(h, 1)]
        gain = gain_ref[pl.ds(h, 1)]
        state = entry_ref[0, h].T
        for b in range(blocks):
            at = slice(b * BLOCK, (b + 1) * BLOCK)
            q, p, v, y = [balanced[at, a * LANES : (a + 1) * LANES] for a in range(4)]
            v_exact = v.astype(BF)
            sig = jax.nn.sigmoid(p)
            forget = bound + (1.0 - bound) * sig
            store = 1.0 - forget
            decay = dot(lower3, cat(thirds(jnp.log(forget)), 0), NN)
            total = decay[BLOCK - 1 : BLOCK]
            eq = jnp.exp(decay)
            ek = jnp.exp(-decay)
            tail = jnp.exp(total - decay) * last_ref[b]
            factor = through_ref[pl.ds(b, 1)] * jnp.exp(total)
            qd = q * eq
            kd = store * ek
            qd2 = halves(qd)
            kd2 = halves(kd)
            scores = nt3(qd2, kd2) * shared_ref[b]
            out = nn2(halves(scores), v_exact) + valid_ref[b] * nt3(qd2, halves(state))
            square_ref[at] += out * out
            cross_ref[at] += gain * y * out
            state_ref[h, b] = state
            state = state * factor + exact_nn2(v.T.astype(BF), halves(store * tail))
            q_bal[h, b] = q.astype(BF)
            v_bal[h, b] = v_exact
            y_bal[h, b] = y.astype(BF)
            sig_ref[h, b] = sig
            forget_ref[h, b] = forget
            store_ref[h, b] = store
            eq_ref[h, b] = eq
            ek_ref[h, b] = ek
            tail_ref[h, b] = tail
            qd_ref[h, b, 0], qd_ref[h, b, 1] = qd2
            kd_ref[h, b, 0], kd_ref[h, b, 1] = kd2
            score_ref[h, b] = scores
            factor_ref[h, b] = factor
            out_ref[h, b] = out
        state_ref[h, blocks] = state
        return carry

    def pair(ref, h, b):
        return ref[h, b, 0], ref[h, b, 1]

    def ahead(h, carry):
        gain = gain_ref[pl.ds(h, 1)]
        for b in range(blocks):
            v_exact = v_bal[h, b]
            kd2 = pair(kd_ref, h, b)
            state2 = halves(state_ref[h, b])
            score_t_ref[h, b, 0], score_t_ref[h, b, 1] = halves(score_ref[h, b].T)
            for value, weight_ref, query_ref, turned_ref in (
                (gain * y_bal[h, b].astype(F32), up_weight_ref, up_query_ref, up_t_ref),
                (out_ref[h, b], out_weight_ref, out_query_ref, out_t_ref),
            ):
                value2 = halves(value)
                weights = nt2(value2, v_exact) * shared_ref[b]
                query_ref[h, b] = eq_ref[h, b] * (
                    nn3(halves(weights), kd2) + valid_ref[b] * nn3(value2, state2)
                )
                weight_ref[h, b] = weights.T
                turned_ref[h, b] = (value * valid_ref[b]).T
        return carry

    for number, (first, past) in enumerate(chunks):
        arrive()
        lax.fori_loop(first, past, forward, 0)
        if number + 1 < len(chunks):
            lax.fori_loop(first, past, ahead, 0)

    ones = jnp.ones((8, 3 * LANES), BF)
    squares = dot(ones, cat(thirds(square_ref[...]), 1), NT)
    crosses = dot(ones, cat(thirds(cross_ref[...]), 1), NT)
    stat_send[...] = jnp.where(iota((8, rows), 0) < 4, squares, crosses)

    def share(k, carry):
        pltpu.make_async_remote_copy(
            src_ref=stat_send,
            dst_ref=stat_recv.at[plane],
            send_sem=send_sem.at[STAT],
            recv_sem=recv_sem.at[STAT],
            device_id={"head": lax.rem(plane + k, head_count)},
            device_id_type=MESH,
        ).start()
        return carry

    lax.fori_loop(1, head_count, share, 0)
    if head_count > 1:
        planes = stat_recv.at[pl.ds(0, head_count - 1)]
        note(planes, planes, STAT)
    stat_recv[plane] = stat_send[...]
    lax.fori_loop(chunks[-1][0], chunks[-1][1], ahead, 0)
    sum_send[...] = jnp.zeros_like(sum_send)
    if head_count > 1:
        arrive()
    stats = jnp.sum(stat_recv[...], axis=0)
    width = float(head_count * heads * LANES)
    inverse = lax.rsqrt(stats[0:1] / width + EPSILON)
    slope = inverse * inverse * inverse * (stats[4:5] / width)
    square_ref[...] = column(inverse)
    cross_ref[...] = column(slope)
    scale_ref[0:1] = inverse
    scale_ref[1:2] = slope

    def mixed_t(up_part, out_part, b):
        at = slice(b * BLOCK, (b + 1) * BLOCK)
        return scale_ref[0:1, at] * up_part - scale_ref[1:2, at] * out_part

    first_member = lax.div(me, group) * group
    mine = lax.rem(me, group)
    groups = count // group
    members = pl.ds(0, group - 1)

    def to_members(view, sem):
        def give(k, carry):
            m = lax.rem(mine + k, group)
            to_ctx(*view(m), sem, first_member + m).start()
            return carry

        lax.fori_loop(1, group, give, 0)

    waves = ((0, 1), (1, heads))
    for w, (first, past) in enumerate(waves):

        def summarize(h, carry):
            back = []
            for b in range(blocks):
                turned = mixed_t(up_t_ref[h, b], out_t_ref[h, b], b)
                back.append(nn3(halves(turned), pair(qd_ref, h, b)))
                back_state_ref[h, b] = back[b]
            summary = back[blocks - 1]
            decay = factor_ref[h, blocks - 1]
            for b in reversed(range(blocks - 1)):
                summary = back[b] + factor_ref[h, b] * summary
                decay = decay * factor_ref[h, b]
            sum_send[:, h + w] = summary.reshape(group, part, LANES)
            sum_send[:, past + w, pl.ds(h - first, 1)] = jnp.broadcast_to(
                decay[None], (group, 1, LANES)
            )
            return carry

        lax.fori_loop(first, past, summarize, 0)
        planes_of = pl.ds(first + w, past - first + 1)
        to_members(
            lambda m: (sum_send.at[m, planes_of], sum_recv.at[mine, planes_of]), SUM + w
        )
        note(sum_send.at[members, planes_of], sum_recv.at[members, planes_of], SUM + w)
    sum_recv[mine] = sum_send[mine]

    def query_side(h, carry):
        parts = []
        for b in range(blocks):
            at = slice(b * BLOCK, (b + 1) * BLOCK)
            dq = square_ref[at] * up_query_ref[h, b] - cross_ref[at] * out_query_ref[h, b]
            dq_bal[h, b] = dq
            parts.append(dq.astype(BF))
        away = dot(back_ref[...], cat(parts, 0), NN)
        dq_send[h] = away.reshape(count, cap, LANES).astype(BF)
        dq_recv[h, me] = dq_send[h, me]
        return carry

    def query_part(first, past, sem):
        span = pl.ds(first, past - first)
        spread(
            me,
            count,
            lambda d: to_ctx(dq_send.at[span, d], dq_recv.at[span, me], sem, d).start(),
        )
        leaving.append((dq_send.at[span, others], sem))
        return dq_recv.at[span, others], sem

    cuts = [0, heads - 2, heads - 1, heads]
    lax.fori_loop(cuts[0], cuts[1], query_side, 0)
    dq_due = [query_part(cuts[0], cuts[1], DQ)]

    def one_back(m, h, w, total):
        first, past = waves[w]
        return sum_recv[m, h + w] + sum_recv[m, past + w, pl.ds(h - first, 1)] * total

    for w, (first, past) in enumerate(waves):
        arrive()

        def scan(h, carry):
            total = jnp.zeros((part, LANES), F32)
            for m in reversed(range(group)):
                total = one_back(m, h, w, total)
            tot_send[h] = total
            return carry

        lax.fori_loop(first, past, scan, 0)
        if groups > 1:
            span = pl.ds(first, past - first)
            before_me = lax.rem(me + count - group, count)
            to_ctx(tot_send.at[span], tot_recv.at[span], TOT + w, before_me).start()
            note(tot_send.at[span], tot_recv.at[span], TOT + w)
    lax.fori_loop(cuts[1], cuts[2], query_side, 0)
    dq_due.append(query_part(cuts[1], cuts[2], DQ + 1))

    for w, (first, past) in enumerate(waves):
        if groups > 1:
            arrive()

        def carries(h, carry):
            if groups > 1:
                total = tot_recv[h] * jnp.where(first_member + group == count, 0.0, 1.0)
            else:
                total = jnp.zeros((part, LANES), F32)
            for m in reversed(range(group)):
                car_send[m, h] = total
                total = one_back(m, h, w, total)
            return carry

        lax.fori_loop(first, past, carries, 0)
        span = pl.ds(first, past - first)
        to_members(lambda m: (car_send.at[m, span], car_recv.at[mine, span]), CAR + w)
        note(car_send.at[members, span], car_recv.at[members, span], CAR + w)
    car_recv[mine] = car_send[mine]
    lax.fori_loop(cuts[2], cuts[3], query_side, 0)
    dq_due.append(query_part(cuts[2], cuts[3], DQ + 2))

    def key_side(h, carry):
        gain = gain_ref[pl.ds(h, 1)]
        for b in range(blocks):
            at = slice(b * BLOCK, (b + 1) * BLOCK)
            g = square_ref[at] * (gain * y_bal[h, b].astype(F32)) - cross_ref[at] * out_ref[h, b]
            weights = mixed_t(up_weight_ref[h, b], out_weight_ref[h, b], b)
            dk_bal[h, b] = ek_ref[h, b] * nn3(halves(weights), pair(qd_ref, h, b))
            dv_bal[h, b] = nn3(pair(score_t_ref, h, b), halves(g))
        return carry

    def finish(h, carry):
        bound = bound_ref[pl.ds(h, 1)]
        incoming = car_recv[:, h].reshape(LANES, LANES)
        pairs = [None] * blocks
        for b in reversed(range(blocks)):
            incoming2 = halves(incoming)
            tail = tail_ref[h, b]
            store = store_ref[h, b]
            sig = sig_ref[h, b]
            dv = dv_bal[h, b] + nt3(halves(store * tail), incoming2)
            dk = dk_bal[h, b] + tail * exact_nn2(v_bal[h, b], incoming2)
            mixture = q_bal[h, b].astype(F32) * dq_bal[h, b] - store * dk
            reach = shared_t_ref[b].astype(BF)
            slope = dot(cat([reach, reach, reach], 1), cat(thirds(mixture), 0), NN)
            slope = slope + last_ref[b] * jnp.sum(
                incoming * state_ref[h, b + 1], axis=0, keepdims=True
            )
            dp = (slope / forget_ref[h, b] - dk) * (1.0 - bound) * sig * (1.0 - sig)
            pairs[b] = cat([dv.astype(BF), dp.astype(BF)], 1)
            if b:
                incoming = back_state_ref[h, b] + factor_ref[h, b] * incoming
        away = dot(back_ref[...], cat(pairs, 0), NN)
        slab = cat(
            [away[:, a * LANES : (a + 1) * LANES].reshape(count, cap, LANES) for a in range(2)],
            1,
        )
        dvp_send[h] = slab.astype(BF)
        dvp_recv[h, me] = dvp_send[h, me]
        return carry

    for w, wave in enumerate(waves):
        lax.fori_loop(*wave, key_side, 0)
        arrive()
        for number, (first, past) in enumerate(chunks):
            if first < wave[0] or first >= wave[1]:
                continue
            lax.fori_loop(first, past, finish, 0)
            span = pl.ds(first, past - first)
            spread(
                me,
                count,
                lambda d: to_ctx(
                    dvp_send.at[span, d], dvp_recv.at[span, me], DVP + number, d
                ).start(),
            )
            note(dvp_send.at[span, others], dvp_recv.at[span, others], DVP + number)
    due[0:0] = dq_due

    def settle_query(h, carry):
        slab = dq_recv[h].astype(F32).reshape(slots, LANES).astype(BF)
        at = pl.ds(pl.multiple_of(h * LANES, LANES), LANES)
        grad_ref[0, :, at] = dot(settle_ref[...], slab, NN).astype(BF)
        return carry

    for first, past in zip(cuts[:-1], cuts[1:]):
        arrive()
        lax.fori_loop(first, past, settle_query, 0)

    def settle(h, carry):
        rows_home = dot(settle_ref[...], unslab(dvp_recv[h], 2), NN).astype(BF)
        at = pl.ds(pl.multiple_of(h * LANES, LANES), LANES)
        grad_ref[2, :, at] = rows_home[:, :LANES]
        grad_ref[1, :, at] = rows_home[:, LANES:]
        return carry

    for number, (first, past) in enumerate(chunks):
        arrive()
        lax.fori_loop(first, past, settle, 0)

    for view, sem in leaving:
        drain(view, send_sem, sem)


def unstack(grad_ref, dq_ref, dp_ref, dv_ref, held, sem):
    outs = (dq_ref, dp_ref, dv_ref)
    loads = [
        pltpu.make_async_copy(grad_ref.at[a], held.at[a], sem.at[a]) for a in range(3)
    ]
    stores = [
        pltpu.make_async_copy(held.at[a], outs[a], sem.at[3 + a]) for a in range(3)
    ]
    for load in loads:
        load.start()
    for load, store in zip(loads, stores):
        load.wait()
        store.start()
    for store in stores:
        store.wait()


def body(
    count,
    head_count,
    query_rows,
    gate_rows,
    value_rows,
    upstream_rows,
    row_map,
    doc_lengths,
    entry_state,
    lower_bound,
    norm_gain,
):
    rows = row_map.shape[0]
    heads = entry_state.shape[1]
    cap = 2 * rows // count
    slots = count * cap
    blocks = rows // BLOCK
    group = DOC_MOST // rows
    chunks = tuple((h, h + 1) for h in range(heads))
    sizes = (count, head_count, rows, heads, cap, group, chunks)
    part = LANES // group
    vmem = pltpu.VMEM
    per_block = (heads, blocks, BLOCK, LANES)
    split_block = (heads, blocks, 2, BLOCK, LANES)
    semaphores = 11 + 2 * len(chunks)
    scratch = [vmem(query_rows.shape, BF) for _ in range(4)] + [
        vmem(entry_state.shape, F32),
        pltpu.SemaphoreType.DMA((5,)),
        vmem((count, 1, LANES), F32),
        vmem((count, 1, LANES), F32),
        vmem((heads, count, 4 * cap, LANES), BF),
        vmem((heads, count, 4 * cap, LANES), BF),
        vmem((heads, count, cap, LANES), BF),
        vmem((heads, count, cap, LANES), BF),
        vmem((heads, count, 2 * cap, LANES), BF),
        vmem((heads, count, 2 * cap, LANES), BF),
        vmem((group, heads + 2, part, LANES), F32),
        vmem((group, heads + 2, part, LANES), F32),
        vmem((heads, part, LANES), F32),
        vmem((heads, part, LANES), F32),
        vmem((group, heads, part, LANES), F32),
        vmem((group, heads, part, LANES), F32),
        vmem((8, rows), F32),
        vmem((head_count, 8, rows), F32),
        vmem((slots, rows), BF),
        vmem((rows, slots), BF),
        vmem((rows, slots), BF),
        vmem((slots, rows), BF),
        vmem((blocks, BLOCK, BLOCK), F32),
        vmem((blocks, BLOCK, BLOCK), F32),
        vmem((blocks, BLOCK, LANES), F32),
        vmem((blocks, BLOCK, LANES), F32),
        vmem((blocks, LANES), F32),
        vmem(per_block, BF),
        vmem(per_block, BF),
        vmem(per_block, BF),
        vmem(per_block, F32),
        vmem(per_block, F32),
        vmem(per_block, F32),
        vmem(per_block, F32),
        vmem(per_block, F32),
        vmem(per_block, F32),
        vmem(split_block, BF),
        vmem(split_block, BF),
        vmem(per_block, F32),
        vmem(split_block, BF),
        vmem(per_block, F32),
        vmem(per_block, F32),
        vmem(per_block, F32),
        vmem(per_block, F32),
        vmem(per_block, F32),
        vmem(per_block, F32),
        vmem((2, rows), F32),
        vmem((heads, blocks + 1, LANES, LANES), F32),
        vmem((heads, blocks, 1, LANES), F32),
        vmem((heads, blocks, LANES, LANES), F32),
        vmem(per_block, F32),
        vmem(per_block, F32),
        vmem(per_block, F32),
        vmem(per_block, F32),
        vmem((rows, LANES), F32),
        vmem((rows, LANES), F32),
        pltpu.SemaphoreType.DMA((semaphores,)),
        pltpu.SemaphoreType.DMA((semaphores,)),
    ]
    whole = pl.BlockSpec(memory_space=pltpu.VMEM)
    anywhere = pl.BlockSpec(memory_space=pl.ANY)
    shape = jax.ShapeDtypeStruct(query_rows.shape, BF)
    grads = pl.pallas_call(
        functools.partial(kernel, sizes),
        out_shape=jax.ShapeDtypeStruct((3,) + query_rows.shape, BF),
        in_specs=[whole] * 2 + [anywhere] * 5 + [whole] * 2,
        out_specs=whole,
        scratch_shapes=scratch,
        compiler_params=pltpu.CompilerParams(
            collective_id=0, has_side_effects=True, vmem_limit_bytes=56 << 20
        ),
    )(
        row_map.reshape(blocks, LANES),
        doc_lengths.reshape(1, doc_lengths.shape[0]),
        query_rows,
        gate_rows,
        value_rows,
        upstream_rows,
        entry_state,
        lower_bound.reshape(heads, LANES),
        norm_gain.reshape(heads, LANES),
    )
    return pl.pallas_call(
        unstack,
        out_shape=(shape, shape, shape),
        in_specs=[anywhere],
        out_specs=(anywhere,) * 3,
        scratch_shapes=[
            pltpu.VMEM((3,) + query_rows.shape, BF),
            pltpu.SemaphoreType.DMA((6,)),
        ],
    )(grads)


def solution(mesh):
    placed = (
        P("ctx", "head"),
        P("ctx", "head"),
        P("ctx", "head"),
        P("ctx", "head"),
        P("ctx"),
        P(),
        P("ctx", "head", None, None),
        P("head"),
        P("head"),
    )
    return jax.shard_map(
        functools.partial(body, mesh.shape["ctx"], mesh.shape["head"]),
        mesh=mesh,
        in_specs=placed,
        out_specs=(P("ctx", "head"), P("ctx", "head"), P("ctx", "head")),
        check_vma=False,
    )
```
